32 devices in a mesh: dat: 4 (over z), seq: 8 (over y, x, core).
Axes of the slice: x: 2, y: 2, z: 4, core: 2. Of those that a mesh axis runs over, the one named last changes fastest.
Arguments:
- clip_latents: bfloat16 [8, 16, 256, 384], P('dat', 'seq'), may hold values from -6 to 6
- conditioning: bfloat16 [8, 384], P('dat'), may hold values from -6 to 6
- timesteps: int32 [8], P('dat'), may hold values from 0 to 999
- clip_live: int32 [8], P('dat'), may hold values 0 or 1
- cotangent: bfloat16 [8, 16, 256, 384], P('dat', 'seq'), may hold values from -6 to 6
- ada_weight: bfloat16 [2, 384, 2304], P(None, ('dat', 'seq')), may hold values from -0.3125 to 0.3125
- query_key_value_weight: bfloat16 [2, 384, 1152], P(None, ('dat', 'seq')), may hold values from -0.3125 to 0.3125
- output_projection_weight: bfloat16 [2, 384, 384], P(None, ('dat', 'seq')), may hold values from -1.25 to 1.25
- first_feedforward_weight: bfloat16 [2, 384, 1536], P(None, ('dat', 'seq')), may hold values from -0.3125 to 0.3125
- second_feedforward_weight: bfloat16 [2, 1536, 384], P(None, ('dat', 'seq')), may hold values from -0.15625 to 0.15625
- biases: bfloat16 [2, 5376], P(None, ('dat', 'seq')), may hold values from -3 to 3
Outputs:
- out_latents: float32 [8, 16, 256, 384], P('dat', 'seq')
- grad_latents: float32 [8, 16, 256, 384], P('dat', 'seq')
- grad_conditioning: float32 [8, 384], P('dat')
- grad_ada: float32 [2, 384, 2304], P(None, ('dat', 'seq'))
- grad_qkv: float32 [2, 384, 1152], P(None, ('dat', 'seq'))
- grad_proj: float32 [2, 384, 384], P(None, ('dat', 'seq'))
- grad_fc1: float32 [2, 384, 1536], P(None, ('dat', 'seq'))
- grad_fc2: float32 [2, 1536, 384], P(None, ('dat', 'seq'))
- grad_biases: float32 [2, 5376], P(None, ('dat', 'seq'))
The draws below stay inside these ranges and needn't reach their ends.
All inputs are finite; a program needn't handle non-finite values. No bound on the sum of `clip_live` on one device may be relied on, other than what follows from the above.
Results may differ from the reference program's by a relative error of at most 0.025.
The reference program's roundings to bfloat16 on the way count: a program that leaves them out, or rounds other values in their place, can miss the bound.
Values may be sent and summed in bfloat16 or wider, within the bound.
No kernel may reach another device: no remote copies, remote signals or barrier semaphores. Data moves between devices by JAX's collectives and lax.ppermute only.
A program may use at most 128 MiB of HBM per device.

```python
import math
import jax
import jax.numpy as jnp
from jax import lax

D = 384
H = 6
HD = 64
FF = 1536
F = 16
P_SIZE = 256
L = 2
TSTEPS = 1000
SLOTS = 8
BIAS = 5376


def touch_ends(values, own_key, low, top_value):
    extent = values.shape
    index_at = [jax.random.randint(jax.random.fold_in(own_key, axis), (), 0, extent[axis]) for axis in range(len(extent))]
    values = values.at[tuple(index_at)].set(low)
    longest = extent.index(max(extent))
    index_at[longest] = (index_at[longest] + 1) % extent[longest]
    return values.at[tuple(index_at)].set(top_value)


def block_scale(rng, extent, cuts, least, largest):
    def one(dim, shards_of):
        draws = jax.random.uniform(jax.random.fold_in(jax.random.fold_in(rng, 6), dim), (shards_of,), jnp.float32, least / len(cuts), largest / len(cuts))
        return jnp.repeat(jnp.exp(draws), extent[dim] // shards_of).reshape((-1,) + (1,) * (len(extent) - dim - 1))

    gain = one(*cuts[0])
    for cut in cuts[1:]:
        gain = gain * one(*cut)
    return gain


def scatter_about(rng, dims, scale, reach, shards=(), kind=jnp.bfloat16):
    factor_of = block_scale(rng, dims, shards, -0.22, 0.18) if shards else 1.0
    drawn = jax.random.normal(rng, dims, jnp.float32) * scale * factor_of
    return jnp.minimum(jnp.maximum(drawn, -reach), reach).astype(kind)


def setup_inputs(seed: int = 0) -> dict:
    key_list = jax.random.split(jax.random.key(seed), 12)
    clip_latents = scatter_about(key_list[0], (SLOTS, F, P_SIZE, D), 1.0, 6.0, ((0, 4), (1, 8)))
    conditioning = scatter_about(key_list[1], (SLOTS, D), 1.0, 6.0, ((0, 4),))
    timesteps = touch_ends(jax.random.randint(key_list[2], (SLOTS,), 0, TSTEPS), jax.random.fold_in(key_list[2], 1), 0, TSTEPS - 1).astype(jnp.int32)
    clip_live = touch_ends((jax.random.randint(key_list[3], (SLOTS,), 0, 4) < 3).astype(jnp.int32), jax.random.fold_in(key_list[3], 1), 0, 1)
    cotangent = scatter_about(key_list[4], (SLOTS, F, P_SIZE, D), 1.0, 6.0, ((0, 4), (1, 8)))
    ada_weight = scatter_about(key_list[5], (L, D, 6 * D), D ** -0.5, 0.3125, ((1, 32),))
    query_key_value_weight = scatter_about(key_list[6], (L, D, 3 * D), D ** -0.5, 0.3125, ((1, 32),))
    output_projection_weight = scatter_about(key_list[7], (L, D, D), (D // 16) ** -0.5, 1.25, ((1, 32),))
    first_feedforward_weight = scatter_about(key_list[8], (L, D, FF), D ** -0.5, 0.3125, ((1, 32),))
    second_feedforward_weight = scatter_about(key_list[9], (L, FF, D), FF ** -0.5, 0.15625, ((1, 32),))
    biases = scatter_about(key_list[10], (L, BIAS), 0.5, 3.0, ((1, 32),))
    return {"clip_latents": clip_latents, "conditioning": conditioning, "timesteps": timesteps, "clip_live": clip_live, "cotangent": cotangent, "ada_weight": ada_weight, "query_key_value_weight": query_key_value_weight, "output_projection_weight": output_projection_weight, "first_feedforward_weight": first_feedforward_weight, "second_feedforward_weight": second_feedforward_weight, "biases": biases}


@jax.custom_vjp
def low(v):
    return lax.optimization_barrier(v.astype(jnp.bfloat16)).astype(jnp.float32)

@jax.custom_vjp
def low_back(v):
    return v

def low_keep(v):
    return (low(v), None)

def low_pass(kept, grad):
    return (grad,)

def back_keep(v):
    return (v, None)

def back_low(kept, grad):
    return (low(grad),)
low.defvjp(low_keep, low_pass)
low_back.defvjp(back_keep, back_low)
highest = lax.Precision.HIGHEST
ln_epsilon = 1e-06

def layer_norm(values):
    center = values - lax.optimization_barrier(jnp.mean(values, axis=-1, keepdims=True))
    spread = lax.optimization_barrier(jnp.mean(center * center, axis=-1, keepdims=True))
    return center * lax.rsqrt(spread + ln_epsilon)

def timestep_embed(timestep, features):
    half_count = features // 2
    frequency = jnp.exp(-math.log(10000.0) * jnp.arange(half_count, dtype=jnp.float32) / half_count)
    angles = timestep.astype(jnp.float32) * frequency
    return jnp.concatenate([jnp.cos(angles), jnp.sin(angles)])

def attend_block(query, key_heads, value_heads):
    scores = low_back(jnp.einsum('shd,thd->hst', query, key_heads, precision=highest) / math.sqrt(HD))
    attn_probs = jax.nn.softmax(scores, axis=-1)
    return jnp.einsum('hst,thd->shd', low(attn_probs), value_heads, precision=highest)

def diffusion_transformer_block(residual_stream, adaptive_modulation, block_weight_set, temporal_layer_flag):
    query_key_value_weight, output_projection_weight, first_feedforward_weight, second_feedforward_weight, bias_vector_row = block_weight_set
    shift_a, scale_a, gate_a, shift_b, scale_b, gate_b = jnp.split(adaptive_modulation, 6)
    token_rows = residual_stream.reshape(F * P_SIZE, D)
    normed_a = low(layer_norm(token_rows) * (1.0 + scale_a) + shift_a)
    query_bias = bias_vector_row[6 * D:7 * D]
    value_bias = bias_vector_row[7 * D:8 * D]
    qkv_bias = jnp.concatenate([query_bias, jnp.zeros_like(query_bias), value_bias])
    projected = low(low_back(jnp.dot(normed_a, query_key_value_weight, precision=highest) + qkv_bias))
    heads_all = projected.reshape(F, P_SIZE, 3, H, HD)
    query, key_heads, value_heads = (heads_all[:, :, 0], heads_all[:, :, 1], heads_all[:, :, 2])
    if temporal_layer_flag:
        order = (1, 0, 2, 3)
        attended = jax.checkpoint(jax.vmap(attend_block))(jnp.transpose(query, order), jnp.transpose(key_heads, order), jnp.transpose(value_heads, order))
        attended = jnp.transpose(attended, order)
    else:
        attended = lax.map(jax.checkpoint(lambda group: attend_block(group[0], group[1], group[2])), (query, key_heads, value_heads))
    attended = low(low_back(attended.reshape(F * P_SIZE, D)))
    branch = low_back(jnp.dot(attended, output_projection_weight, precision=highest) + bias_vector_row[8 * D:9 * D])
    midway = token_rows + gate_a * branch
    normed_b = low(layer_norm(midway) * (1.0 + scale_b) + shift_b)
    hidden_pre = low_back(jnp.dot(normed_b, first_feedforward_weight, precision=highest) + bias_vector_row[9 * D:9 * D + FF])
    hidden_act = low(jax.nn.gelu(hidden_pre, approximate=True))
    mlp_out = low_back(jnp.dot(hidden_act, second_feedforward_weight, precision=highest) + bias_vector_row[9 * D + FF:])
    return (midway + gate_b * mlp_out).reshape(F, P_SIZE, D)

def clip_forward(latents, cond_vec, timestep, params):
    cond_act = low(jax.nn.silu(cond_vec + timestep_embed(timestep, D)))
    residual_stream = latents
    for layer_position_index in range(L):
        ada_weight, query_key_value_weight, output_projection_weight, first_feedforward_weight, second_feedforward_weight, bias_vector_row = [member[layer_position_index] for member in params]
        adaptive_modulation = jnp.dot(cond_act, ada_weight, precision=highest) + bias_vector_row[:6 * D]
        residual_stream = diffusion_transformer_block(residual_stream, adaptive_modulation, (query_key_value_weight, output_projection_weight, first_feedforward_weight, second_feedforward_weight, bias_vector_row), layer_position_index % 2 == 1)
    return residual_stream

def reference(clip_latents, conditioning, timesteps, clip_live, cotangent, ada_weight, query_key_value_weight, output_projection_weight, first_feedforward_weight, second_feedforward_weight, biases):
    params = tuple((member.astype(jnp.float32) for member in (ada_weight, query_key_value_weight, output_projection_weight, first_feedforward_weight, second_feedforward_weight, biases)))

    def per_clip(summed, clip_item):
        latents, cond_vec, timestep, alive_flag, cot_clip = clip_item
        latents = latents.astype(jnp.float32)
        cot_float = cot_clip.astype(jnp.float32)

        def forward(residual_stream, cond_float, block_weight_set):
            return clip_forward(residual_stream, cond_float, timestep, block_weight_set)
        result, pullback = jax.vjp(forward, latents, cond_vec.astype(jnp.float32), params)
        grad_in, grad_cond, grad_params = pullback(cot_float * alive_flag.astype(jnp.float32))
        summed = tuple((acc_term + new_term for acc_term, new_term in zip(summed, grad_params)))
        out_clip = jnp.where(alive_flag > 0, result, latents)
        grad_clip = jnp.where(alive_flag > 0, grad_in, cot_float)
        return (summed, (out_clip, grad_clip, grad_cond))
    initial = tuple((jnp.zeros_like(member) for member in params))
    summed, (out_latents, grad_latents, grad_conditioning) = lax.scan(per_clip, initial, (clip_latents, conditioning, timesteps, clip_live, cotangent))
    return (out_latents, grad_latents, grad_conditioning) + tuple(summed)
```

```python
from functools import partial
import math

import jax
import jax.numpy as jnp
from jax import lax
from jax.experimental import pallas as pl
from jax.experimental.pallas import tpu as pltpu
from jax.sharding import PartitionSpec as P

H = 6
HD = 64
EPS = 1e-06
BF = jnp.bfloat16
F32 = jnp.float32
GELU_A = math.sqrt(2.0 / math.pi)
GELU_B = 0.044715
VMEM_LIMIT = 60 * 1024 * 1024


def dot_nn(a, b):
    return lax.dot_general(a, b, (((1,), (0,)), ((), ())), preferred_element_type=F32)


def dot_nt(a, b):
    return lax.dot_general(a, b, (((1,), (1,)), ((), ())), preferred_element_type=F32)


def dot_tn(a, b):
    return lax.dot_general(a, b, (((0,), (0,)), ((), ())), preferred_element_type=F32)


def normalize(v):
    center = v - jnp.mean(v, axis=-1, keepdims=True)
    rstd = lax.rsqrt(jnp.mean(center * center, axis=-1, keepdims=True) + EPS)
    return center * rstd, rstd


def normalize_back(grad, normed, rstd):
    m1 = jnp.mean(grad, axis=-1, keepdims=True)
    m2 = jnp.mean(grad * normed, axis=-1, keepdims=True)
    return rstd * (grad - m1 - normed * m2)


def column_sum(v):
    return jnp.sum(v.astype(F32), axis=0, keepdims=True)


def gelu_parts(v):
    sq = v * v
    th = jnp.tanh(v * (GELU_A + (GELU_A * GELU_B) * sq))
    half = 0.5 + 0.5 * th
    act = v * half
    slope = half + act * (1.0 - th) * (GELU_A + (3.0 * GELU_A * GELU_B) * sq)
    return act, slope


def head_masks(rows):
    lane = lax.broadcasted_iota(jnp.int32, (rows, 2 * HD), 1)
    return lane < HD, lane >= HD


def pick(mask, v):
    return jnp.where(mask, v, jnp.zeros_like(v))


def attend_tile(projected, width, group, place_mask):
    rows = projected.shape[0]
    masks = head_masks(group)
    scale = 1.0 / math.sqrt(HD)
    blocks, totals = [], []
    for g in range(rows // group):
        part = projected[g * group : (g + 1) * group]
        pairs = []
        for j in range(width // (2 * HD)):
            at = 2 * HD * j
            q2 = part[:, at : at + 2 * HD]
            k2 = part[:, width + at : width + at + 2 * HD]
            v2 = part[:, 2 * width + at : 2 * width + at + 2 * HD]
            out = None
            for mask in masks:
                s = dot_nt(k2, pick(mask, q2)) * scale
                if place_mask is not None:
                    s = jnp.where(place_mask, s, -1e30)
                peak = jnp.max(s, axis=0, keepdims=True)
                e = jnp.exp(s - peak)
                total = jnp.sum(e, axis=0, keepdims=True)
                totals.append(peak + jnp.log(total))
                p = (e * (1.0 / total)).astype(BF)
                term = dot_tn(p, pick(mask, v2))
                out = term if out is None else out + term
            pairs.append(out)
        blocks.append(jnp.concatenate(pairs, axis=1))
    return jnp.concatenate(blocks, axis=0), totals


def attend_back_tile(projected, totals, grad_attended, width, group, place_mask):
    rows = projected.shape[0]
    masks = head_masks(group)
    scale = 1.0 / math.sqrt(HD)
    blocks = []
    index = 0
    for g in range(rows // group):
        part = projected[g * group : (g + 1) * group]
        ga = grad_attended[g * group : (g + 1) * group]
        dqs, dks, dvs = [], [], []
        for j in range(width // (2 * HD)):
            at = 2 * HD * j
            q2 = part[:, at : at + 2 * HD]
            k2 = part[:, width + at : width + at + 2 * HD]
            v2 = part[:, 2 * width + at : 2 * width + at + 2 * HD]
            do2 = ga[:, at : at + 2 * HD]
            dq = dk = dv = None
            for mask in masks:
                qm, dom, km = pick(mask, q2), pick(mask, do2), pick(mask, k2)
                p = jnp.exp(dot_nt(k2, qm) * scale - totals[index])
                if place_mask is not None:
                    p = jnp.where(place_mask, p, 0.0)
                index += 1
                dp = dot_nt(v2, dom)
                rowdot = jnp.sum(dp * p, axis=0, keepdims=True)
                ds = (p * (dp - rowdot)).astype(BF)
                tv = dot_nn(p.astype(BF), dom)
                tk = dot_nn(ds, qm)
                tq = dot_tn(ds, km)
                dv = tv if dv is None else dv + tv
                dk = tk if dk is None else dk + tk
                dq = tq if dq is None else dq + tq
            dqs.append((dq * scale).astype(BF))
            dks.append((dk * scale).astype(BF))
            dvs.append(dv.astype(BF))
        blocks.append(jnp.concatenate(dqs + dks + dvs, axis=1))
    return jnp.concatenate(blocks, axis=0)


def forward_tile(x, mod, bias, weights, group, place_mask):
    wqkv, wo, w1, w2 = weights
    d = x.shape[-1]
    sh_a, sc_a, g_a, sh_b, sc_b, g_b = [mod[i : i + 1] for i in range(6)]
    na, rstd_a = normalize(x)
    normed_a = (na * (1.0 + sc_a) + sh_a).astype(BF)
    projected = (dot_nn(normed_a, wqkv[...]) + bias[:, : 3 * d]).astype(BF)
    attended, totals = attend_tile(projected, d, group, place_mask)
    attended = attended.astype(BF)
    branch = dot_nn(attended, wo[...]) + bias[:, 3 * d : 4 * d]
    step_a = g_a * branch
    mid = x + step_a
    nb, rstd_b = normalize(mid)
    normed_b = (nb * (1.0 + sc_b) + sh_b).astype(BF)
    act, slope = gelu_parts(dot_nn(normed_b, w1[...]) + bias[:, 4 * d : -d])
    act = act.astype(BF)
    slope = slope.astype(BF)
    mlp = dot_nn(act, w2[...]) + bias[:, -d:]
    delta = step_a + g_b * mlp
    kept = dict(
        na=na, rstd_a=rstd_a, mid=mid, normed_a=normed_a, projected=projected, totals=totals,
        attended=attended, branch=branch, nb=nb, rstd_b=rstd_b, normed_b=normed_b,
        act=act, slope=slope, mlp=mlp,
    )
    return delta, kept


def backward_tile(g, mod, kept, weights, sums, group, place_mask):
    wqkv, wo, w1, w2 = weights
    aqkv, ao, a1, a2 = sums
    d = g.shape[-1]
    sh_a, sc_a, g_a, sh_b, sc_b, g_b = [mod[i : i + 1] for i in range(6)]
    gm = (g_b * g).astype(BF)
    t_gate_b = jnp.sum(g * kept["mlp"].astype(F32), axis=0, keepdims=True)
    a2[...] += dot_tn(kept["act"], gm)
    gp = (dot_nt(gm, w2[...]) * kept["slope"].astype(F32)).astype(BF)
    a1[...] += dot_tn(kept["normed_b"], gp)
    gnb = dot_nt(gp, w1[...])
    t_shift_b = jnp.sum(gnb, axis=0, keepdims=True)
    t_scale_b = jnp.sum(gnb * kept["nb"], axis=0, keepdims=True)
    dmid = normalize_back((1.0 + sc_b) * gnb, kept["nb"], kept["rstd_b"])
    gmid = g + dmid
    gbr = (g_a * gmid).astype(BF)
    t_gate_a = jnp.sum(gmid * kept["branch"].astype(F32), axis=0, keepdims=True)
    ao[...] += dot_tn(kept["attended"], gbr)
    ga = dot_nt(gbr, wo[...]).astype(BF)
    gproj = attend_back_tile(kept["projected"], kept["totals"], ga, d, group, place_mask)
    aqkv[...] += dot_tn(kept["normed_a"], gproj)
    gna = dot_nt(gproj, wqkv[...])
    t_shift_a = jnp.sum(gna, axis=0, keepdims=True)
    t_scale_a = jnp.sum(gna * kept["na"], axis=0, keepdims=True)
    dx = dmid + normalize_back((1.0 + sc_a) * gna, kept["na"], kept["rstd_a"])
    mods = [t_shift_a, t_scale_a, t_gate_a, t_shift_b, t_scale_b, t_gate_b]
    biases = [column_sum(gproj), column_sum(gbr), column_sum(gp), column_sum(gm)]
    return dx, mods, jnp.concatenate(biases, axis=1)


def unpack_weights(owner, row_map, parts, weights):
    wqkv, wo, w1, w2 = weights
    d = wo.shape[0]
    n_rows = row_map.shape[1]
    line = lax.broadcasted_iota(jnp.int32, (d, n_rows), 0)
    place = [(line == row_map[i : i + 1, :]).astype(F32).astype(BF) for i in range(4)]

    def columns(at):
        return jnp.concatenate(
            [p[:, :, at : at + d].reshape(-1, d) for p in parts], axis=0
        )

    blocks = [columns(d * c) for c in range(6)]
    wqkv[:, :d] = dot_nn(place[0], blocks[0]).astype(BF)
    for c in range(4):
        w1[:, d * c : d * (c + 1)] = dot_nn(place[0], blocks[1 + c]).astype(BF)
    wo[...] = dot_nn(place[0], blocks[5]).astype(BF)
    for half in range(2):
        total = None
        for t in range(3):
            term = dot_nn(place[1 + t], blocks[2 * t + half])
            total = term if total is None else total + term
        wqkv[:, d * (1 + half) : d * (2 + half)] = total.astype(BF)
    at = 0
    for p in parts:
        for k in range(p.shape[0]):
            base = pl.multiple_of(owner[at + k] * 48, 16)
            for t in range(3):
                w2[pl.ds(base + 16 * t, 16), :] = p[k, :, 6 * d + d * t : 6 * d + d * (t + 1)]
        at += p.shape[0]


def pack_terms(owner, column_map, sums, out):
    aqkv, ao, a1, a2 = sums
    d = ao.shape[0]
    n_rows = column_map.shape[0]
    lane = lax.broadcasted_iota(jnp.int32, (n_rows, d), 1)
    place = [(lane == column_map[:, i : i + 1]).astype(F32).astype(BF) for i in range(4)]
    main = [aqkv[:, :d]] + [a1[:, d * c : d * (c + 1)] for c in range(4)] + [ao[...]]
    rest = [aqkv[:, d * (1 + half) : d * (2 + half)].astype(BF) for half in range(2)]
    for c in range(6):
        block = dot_nn(place[0], main[c].astype(BF)) + dot_nn(place[1 + c // 2], rest[c % 2])
        out[:, :, d * c : d * (c + 1)] = block.astype(BF).reshape(-1, 16, d)
    for k in range(out.shape[0]):
        base = pl.multiple_of(owner[k] * 48, 16)
        for t in range(3):
            out[k, :, 6 * d + d * t : 6 * d + d * (t + 1)] = a2[pl.ds(base + 16 * t, 16), :].astype(BF)


def spatial_forward_kernel(n_parts, owner, row_map, *refs):
    parts, refs = refs[:n_parts], refs[n_parts:]
    x_ref, mod_ref, bias_ref = refs[:3]
    weights = refs[3:7]
    (send, stream, totals, normed_a, projected, attended, branch, mid, normed_b, act,
     slope, mlp) = refs[7:]

    @pl.when(pl.program_id(0) == 0)
    def _():
        unpack_weights(owner, row_map, parts, weights)

    x = x_ref[0, 0].astype(F32)
    delta, kept = forward_tile(x, mod_ref[0], bias_ref[...], weights, x.shape[0], None)
    total = x + delta
    stream[0, 0] = total
    send[...] = total.astype(BF).reshape(send.shape)
    totals[0] = jnp.concatenate(kept["totals"] + [jnp.zeros_like(kept["totals"][0])] * 2, axis=0)
    normed_a[...] = kept["normed_a"]
    projected[...] = kept["projected"]
    attended[...] = kept["attended"]
    branch[...] = kept["branch"].astype(BF)
    mid[...] = kept["mid"]
    normed_b[...] = kept["normed_b"]
    act[...] = kept["act"]
    slope[...] = kept["slope"]
    mlp[...] = kept["mlp"].astype(BF)


def clear(step, refs):
    @pl.when(step)
    def _():
        for r in refs:
            r[...] = jnp.zeros_like(r)


def add_rows(ref, rows, first):
    block = jnp.concatenate(rows + [jnp.zeros_like(rows[0])] * 2, axis=0)
    clear(first, [ref])
    ref[0] += block


def gather_rows(block):
    frames = block.shape[0] * block.shape[2]
    v = block.astype(F32).reshape(frames, block.shape[3], block.shape[4])
    groups = [
        v[:, 8 * b : 8 * (b + 1)].reshape(8 * frames, v.shape[2]) for b in range(v.shape[1] // 8)
    ]
    return jnp.concatenate(groups, axis=0)


def scatter_rows(rows, shape):
    frames = shape[0] * shape[2]
    groups = [
        rows[8 * frames * b : 8 * frames * (b + 1)].reshape(frames, 8, shape[4])
        for b in range(shape[3] // 8)
    ]
    return jnp.concatenate(groups, axis=1).astype(BF).reshape(shape)


def temporal_kernel(n_parts, per_clip, owner, row_map, column_map, *refs):
    parts, refs = refs[:n_parts], refs[n_parts:]
    x_ref, g_ref, mod_ref, bias_ref = refs[:4]
    out_delta, grad_delta, mods, biases, payload = refs[4:9]
    weights, sums = refs[9:13], refs[13:17]
    step = pl.program_id(0)

    @pl.when(step == 0)
    def _():
        unpack_weights(owner, row_map, parts, weights)

    clear(step == 0, list(sums) + [biases])
    x = gather_rows(x_ref[...])
    g = gather_rows(g_ref[...])
    group = 8 * x_ref.shape[0] * x_ref.shape[2]
    row = lax.broadcasted_iota(jnp.int32, (group, group), 0)
    lane = lax.broadcasted_iota(jnp.int32, (group, group), 1)
    place_mask = ((row ^ lane) & 7) == 0
    mod = mod_ref[0]
    delta, kept = forward_tile(x, mod, bias_ref[...], weights, group, place_mask)
    out_delta[...] = scatter_rows(delta, out_delta.shape)
    dx, mod_rows, bias_row = backward_tile(g, mod, kept, weights, sums, group, place_mask)
    grad_delta[...] = scatter_rows(dx, grad_delta.shape)
    add_rows(mods, mod_rows, step % per_clip == 0)
    biases[...] += bias_row

    @pl.when(step == pl.num_programs(0) - 1)
    def _():
        pack_terms(owner, column_map, sums, payload)


def spatial_backward_kernel(per_clip, owner, live, column_map, *refs):
    x_ref, cot_ref, gd_ref, mod_ref = refs[:4]
    weights = refs[4:8]
    totals, normed_a, projected, attended, branch, mid, normed_b, act, slope, mlp = refs[8:18]
    grad_out, mods, biases, payload = refs[18:22]
    sums = refs[22:26]
    step = pl.program_id(0)
    clear(step == 0, list(sums) + [biases])
    alive = live[step // per_clip].astype(F32)
    cot = cot_ref[0, 0].astype(F32)
    g = cot * alive + gd_ref[...].astype(F32).reshape(cot.shape)
    mod = mod_ref[0]
    na, rstd_a = normalize(x_ref[0, 0].astype(F32))
    nb, rstd_b = normalize(mid[...])
    kept = dict(
        na=na, rstd_a=rstd_a, nb=nb, rstd_b=rstd_b, normed_a=normed_a[...],
        projected=projected[...], totals=[totals[0, h : h + 1] for h in range(H)],
        attended=attended[...], branch=branch[...], normed_b=normed_b[...],
        act=act[...], slope=slope[...], mlp=mlp[...],
    )
    dx, mod_rows, bias_row = backward_tile(g, mod, kept, weights, sums, cot.shape[0], None)
    grad_out[0, 0] = jnp.where(alive > 0, g + dx, cot)
    add_rows(mods, mod_rows, step % per_clip == 0)
    biases[...] += bias_row

    @pl.when(step == pl.num_programs(0) - 1)
    def _():
        pack_terms(owner, column_map, sums, payload)


def whole(a):
    zeros = (0,) * len(a.shape)
    return pl.BlockSpec(a.shape, lambda t: zeros, pipeline_mode=pl.Buffered(1))


def smem():
    return pl.BlockSpec(memory_space=pltpu.SMEM)


def shape(dims, dtype):
    return jax.ShapeDtypeStruct(dims, dtype)


PARAMS = pltpu.CompilerParams(
    dimension_semantics=("arbitrary",), vmem_limit_bytes=VMEM_LIMIT
)


def weight_shapes(d, ff, make):
    return [make((d, 3 * d)), make((d, d)), make((d, ff)), make((ff, d))]


def spatial_forward(owner, row_map, parts, x, mod, bias):
    clips, frames, places, d = x.shape
    ff = bias.shape[1] - 5 * d
    dests = lax.axis_size("seq")
    tiles = clips * frames
    rows = tiles * places
    tile4 = pl.BlockSpec((1, 1, places, d), lambda t: (t // frames, t % frames, 0, 0))

    def row_block(cols):
        return pl.BlockSpec((places, cols), lambda t: (t, 0))

    outs = [shape((d, 3 * d), BF), shape((d, d), BF), shape((d, ff), BF), shape((ff, d), BF)]
    specs = [whole(o) for o in outs]
    outs += [shape((dests, clips, frames, places // dests, d), BF), shape(x.shape, F32),
             shape((tiles, 8, places), F32)]
    specs += [
        pl.BlockSpec((dests, 1, 1, places // dests, d), lambda t: (0, t // frames, t % frames, 0, 0)),
        tile4, pl.BlockSpec((1, 8, places), lambda t: (t, 0, 0)),
    ]
    for cols, dtype in ((d, BF), (3 * d, BF), (d, BF), (d, BF), (d, F32), (d, BF), (ff, BF), (ff, BF), (d, BF)):
        outs.append(shape((rows, cols), dtype))
        specs.append(row_block(cols))
    return pl.pallas_call(
        partial(spatial_forward_kernel, len(parts)),
        grid=(tiles,),
        in_specs=[smem(), whole(row_map)] + [whole(p) for p in parts]
        + [tile4, pl.BlockSpec((1, 8, d), lambda t: (t // frames, 0, 0)), whole(bias)],
        out_specs=specs,
        out_shape=outs,
        compiler_params=PARAMS,
        name="spatial_forward",
    )(owner, row_map, *parts, x, mod, bias)


def temporal_block(owner, row_map, column_map, parts, x, g, mod, bias):
    sources, clips, frames, places, d = x.shape
    ff = bias.shape[1] - 5 * d
    span = 16
    per_clip = places // span
    tile = pl.BlockSpec(
        (sources, 1, frames, span, d), lambda t: (0, t // per_clip, 0, t % per_clip, 0)
    )
    mod_spec = pl.BlockSpec((1, 8, d), lambda t: (t // per_clip, 0, 0))
    n = owner.shape[0]
    outs = [shape(x.shape, BF), shape(x.shape, BF), shape((clips, 8, d), F32),
            shape(bias.shape, F32), shape((n, 16, 9 * d), BF)]
    return pl.pallas_call(
        partial(temporal_kernel, len(parts), per_clip),
        grid=(clips * per_clip,),
        in_specs=[smem(), whole(row_map), whole(column_map)] + [whole(p) for p in parts]
        + [tile, tile, mod_spec, whole(bias)],
        out_specs=[tile, tile, mod_spec, whole(bias), whole(outs[4])],
        out_shape=outs,
        scratch_shapes=weight_shapes(d, ff, lambda s: pltpu.VMEM(s, BF))
        + weight_shapes(d, ff, lambda s: pltpu.VMEM(s, F32)),
        compiler_params=PARAMS,
        name="temporal_block",
    )(owner, row_map, column_map, *parts, x, g, mod, bias)


def spatial_backward(owner, live, column_map, x, cot, grad_delta, mod, weights, saved):
    clips, frames, places, d = x.shape
    ff = weights[3].shape[0]
    dests = grad_delta.shape[0]
    tile4 = pl.BlockSpec((1, 1, places, d), lambda t: (t // frames, t % frames, 0, 0))
    mod_spec = pl.BlockSpec((1, 8, d), lambda t: (t // frames, 0, 0))
    n = owner.shape[0]
    outs = [shape(x.shape, F32), shape((clips, 8, d), F32), shape((1, 5 * d + ff), F32),
            shape((n, 16, 9 * d), BF)]
    return pl.pallas_call(
        partial(spatial_backward_kernel, frames),
        grid=(clips * frames,),
        in_specs=[smem(), smem(), whole(column_map), tile4, tile4,
                  pl.BlockSpec((dests, 1, 1, places // dests, d), lambda t: (0, t // frames, t % frames, 0, 0)),
                  mod_spec] + [whole(w) for w in weights]
        + [pl.BlockSpec((1, 8, places), lambda t: (t, 0, 0))]
        + [pl.BlockSpec((places, s.shape[1]), lambda t: (t, 0)) for s in saved[1:]],
        out_specs=[tile4, mod_spec, whole(outs[2]), whole(outs[3])],
        out_shape=outs,
        scratch_shapes=weight_shapes(d, ff, lambda s: pltpu.VMEM(s, F32)),
        compiler_params=PARAMS,
        name="spatial_backward",
    )(owner, live, column_map, x, cot, grad_delta, mod, *weights, *saved)


def row_maps(owner):
    i = jnp.arange(16, dtype=jnp.int32)[None, :]
    base = 12 * owner[:, None]
    cols = [jnp.where(i < 12, base + i, -1)]
    for t in range(3):
        cols.append(jnp.where(i >= 12, base + 4 * t + i - 12, -1))
    rows = jnp.stack([c.reshape(-1) for c in cols] + [jnp.full((16 * owner.shape[0],), -1, jnp.int32)] * 4)
    return rows, rows.T


def pack_shard(qkv, proj, fc1, fc2):
    d = proj.shape[1]
    main = jnp.concatenate([qkv[:, :d], fc1, proj], axis=1)
    rest = jnp.concatenate([qkv[4 * t : 4 * t + 4, d:] for t in range(3)], axis=1)
    tail = jnp.concatenate([fc2[16 * t : 16 * t + 16] for t in range(3)], axis=1)
    return jnp.concatenate([jnp.concatenate([main, rest], axis=0), tail], axis=1)


def unpack_shard(packed):
    d = packed.shape[1] // 9
    rest = [packed[12:, 2 * d * t : 2 * d * (t + 1)] for t in range(3)]
    qkv = jnp.concatenate([packed[:12, :d], jnp.concatenate(rest, axis=0)], axis=1)
    fc2 = jnp.concatenate([packed[:, 6 * d + d * t : 6 * d + d * (t + 1)] for t in range(3)], axis=0)
    return qkv, packed[:12, 5 * d : 6 * d], packed[:12, d : 5 * d], fc2


AXES = ("dat", "seq")


def swap(v, distance_of):
    pairs = [(i, i ^ distance_of(i)) for i in range(lax.axis_size("dat") * lax.axis_size("seq"))]
    return lax.ppermute(v, AXES, pairs)


def first_hop(i):
    return 4 if i % 2 else 2


def second_hop(i):
    return 2 if i % 2 else 4


def core_hop(i):
    return 1


def exchange(v, axis):
    return lax.all_to_all(v, axis, split_axis=0, concat_axis=0, tiled=True)


def spread(v, axis, size):
    return exchange(jnp.broadcast_to(v[None], (size,) + v.shape), axis)


def chain_owner(dat, me):
    core = me % 2
    p3 = jnp.where(core == 1, 4, 2)
    p4 = jnp.where(core == 1, 2, 4)
    q = me ^ 1
    low = jnp.stack([me, me ^ p3, me ^ p4, me ^ p3 ^ p4, q, q ^ p4, q ^ p3, q ^ p3 ^ p4])
    return (low[:, None] + 8 * jnp.arange(dat)[None, :]).reshape(-1).astype(jnp.int32)


def chain_gather(shard, dat):
    a = spread(shard, "dat", dat)
    b = swap(a, first_hop)
    ab = jnp.concatenate([a, b])
    e1 = swap(ab, core_hop)
    c = swap(ab, second_hop)
    e2 = swap(c, core_hop)
    return [ab, c, e1, e2]


def chain_reduce(payload, dat):
    half = payload.shape[0] // 2

    def step(v, hop):
        m = v.shape[0] // 2
        return (v[:m].astype(F32) + swap(v[m:], hop).astype(F32)).astype(BF)

    v = step(payload, core_hop)
    v = step(v, second_hop)
    v = step(v, first_hop)
    return jnp.sum(exchange(v, "dat").astype(F32), axis=0)


def whole_shards(weights):
    gathered = [lax.all_gather(w, AXES, axis=0, tiled=True) for w in weights]
    count = gathered[0].shape[0] // 12
    return jnp.stack([
        pack_shard(*[w[size * k : size * (k + 1)] for w, size in zip(gathered, (12, 12, 12, 48))])
        for k in range(count)
    ])


def scatter_whole(payload):
    cut = [unpack_shard(payload[k].astype(F32)) for k in range(payload.shape[0])]
    joined = [jnp.concatenate([c[i] for c in cut]) for i in range(4)]
    return [lax.psum_scatter(w, AXES, scatter_dimension=0, tiled=True) for w in joined]


def timestep_embed(timestep, features):
    half_count = features // 2
    frequency = jnp.exp(-math.log(10000.0) * jnp.arange(half_count, dtype=F32) / half_count)
    angles = timestep.astype(F32)[:, None] * frequency
    return jnp.concatenate([jnp.cos(angles), jnp.sin(angles)], axis=1)


def per_device(latents, conditioning, timesteps, live, cotangent, ada, qkv, proj, fc1, fc2, biases):
    dat, seq = lax.axis_size("dat"), lax.axis_size("seq")
    n = dat * seq
    group, place = lax.axis_index("dat"), lax.axis_index("seq")
    index = group * seq + place
    layers, own, wide = ada.shape
    clips, frames, places, d = latents.shape
    fast = dat == 4 and seq == 8 and own == 12
    share = biases.shape[1]
    total_bias = share * n
    part = layers * wide // seq
    highest = lax.Precision.HIGHEST

    alive = live.astype(BF)[:, None, None, None]
    cot_send = (cotangent * alive).reshape(clips, frames, seq, places // seq, d).transpose(2, 0, 1, 3, 4)
    cot_places = exchange(cot_send, "seq")

    if fast:
        shards = [pack_shard(qkv[l], proj[l], fc1[l], fc2[l]) for l in range(layers)]
        parts0 = chain_gather(shards[0], dat)
        owner0 = chain_owner(dat, place)
        parts1 = [lax.all_gather(shards[1], AXES, axis=0)]
        owner1 = jnp.arange(n, dtype=jnp.int32)
    else:
        parts0, parts1 = [[whole_shards([w[l] for w in (qkv, proj, fc1, fc2)])] for l in range(2)]
        owner0 = owner1 = jnp.arange(parts0[0].shape[0], dtype=jnp.int32)
    rows0, cols0 = row_maps(owner0)
    rows1, cols1 = row_maps(owner1)

    cond_total = conditioning.astype(F32) + timestep_embed(timesteps, d)
    cond_act = jax.nn.silu(cond_total).astype(BF)
    cond_all = spread(cond_act, "dat", dat).reshape(dat * clips, d)
    cond_mine = lax.dynamic_slice(cond_all, (0, index * own), (dat * clips, own))
    terms = jnp.einsum("cd,ldm->clm", cond_mine, ada, preferred_element_type=F32)
    terms = terms.reshape(dat, clips, seq, part).transpose(0, 2, 1, 3).reshape(n, clips * part)
    bias_sent = jnp.broadcast_to(biases.astype(F32).reshape(1, layers * share), (n, layers * share))
    got = exchange(jnp.concatenate([terms, bias_sent], axis=1), AXES)
    mod_part = jnp.sum(got[:, : clips * part], axis=0)
    bias_rows = got[:, clips * part :].reshape(n, layers, share).transpose(1, 0, 2).reshape(layers, total_bias)
    mod_all = spread(mod_part, "seq", seq).reshape(seq, clips, part).transpose(1, 0, 2)
    mod_all = mod_all.reshape(clips, layers, wide) + bias_rows[None, :, :wide]
    mod_all = jnp.pad(mod_all.reshape(clips, layers, 6, d), ((0, 0), (0, 0), (0, 2), (0, 0)))
    bias_all = jnp.concatenate(
        [bias_rows[:, wide : wide + d], jnp.zeros((layers, d), F32), bias_rows[:, wide + d :]], axis=1
    )

    outs = spatial_forward(owner0, rows0, parts0, latents, mod_all[:, 0], bias_all[:1])
    weights0, sent, stream, saved = outs[:4], outs[4], outs[5], outs[6:]
    stream_places = exchange(sent, "seq")
    out_delta, grad_delta, mods1, sums1, payload1 = temporal_block(
        owner1, rows1, cols1, parts1, stream_places, cot_places, mod_all[:, 1], bias_all[1:]
    )
    grad_back = exchange(grad_delta, "seq")
    out_back = exchange(out_delta, "seq")
    grad_latents, mods0, sums0, payload0 = spatial_backward(
        owner0, live, cols0, latents, cotangent, grad_back, mod_all[:, 0], weights0, saved
    )
    delta = out_back.transpose(1, 2, 0, 3, 4).reshape(latents.shape).astype(F32)
    out_latents = jnp.where((live > 0)[:, None, None, None], stream + delta, latents.astype(F32))

    if fast:
        flat = payload1.reshape(n * 16, payload1.shape[2])
        share1 = lax.psum_scatter(flat, AXES, scatter_dimension=0, tiled=True).astype(F32)
        share0 = chain_reduce(payload0, dat)
        shares = [unpack_shard(share0), unpack_shard(share1)]
    else:
        shares = [scatter_whole(payload0), scatter_whole(payload1)]
    grads = [jnp.stack([shares[l][i] for l in range(layers)]) for i in range(4)]

    mods = jnp.stack([mods0[:, :6], mods1[:, :6]], axis=1).reshape(clips, seq, part)
    mod_sum = jnp.sum(exchange(mods.transpose(1, 0, 2), "seq"), axis=0)
    sums = jnp.concatenate([sums0, sums1])
    bias_terms = jnp.concatenate(
        [jnp.sum(mods, axis=0).reshape(layers, wide), sums[:, :d], sums[:, 2 * d :]], axis=1
    )
    bias_terms = bias_terms.reshape(layers, n, share).transpose(1, 0, 2).reshape(n, layers * share)
    mod_sent = jnp.broadcast_to(mod_sum.reshape(1, clips * part), (n, clips * part))
    got = exchange(jnp.concatenate([mod_sent, bias_terms], axis=1), AXES)
    grad_biases = jnp.sum(got[:, clips * part :], axis=0).reshape(layers, share)
    mod_total = got[:, : clips * part].reshape(dat, seq, clips, part).transpose(0, 2, 1, 3)
    mod_total = mod_total.reshape(dat * clips, layers, wide)
    grad_ada = jnp.einsum("cd,clm->ldm", cond_mine.astype(F32), mod_total, precision=highest)
    cond_terms = jnp.einsum("clm,ldm->cd", mod_total, ada.astype(F32), precision=highest)
    cond_sent = jnp.broadcast_to(
        cond_terms.reshape(dat, 1, clips, own), (dat, seq, clips, own)
    ).reshape(n, clips, own)
    grad_cond = exchange(cond_sent, AXES).transpose(1, 0, 2).reshape(clips, d)
    grad_conditioning = jax.vjp(jax.nn.silu, cond_total)[1](grad_cond)[0]
    return (out_latents, grad_latents, grad_conditioning, grad_ada, *grads, grad_biases)


def solution(mesh):
    rows = P(None, ("dat", "seq"), None)
    tokens = P("dat", "seq", None, None)
    in_specs = (tokens, P("dat", None), P("dat"), P("dat"), tokens, rows, rows, rows, rows, rows,
                P(None, ("dat", "seq")))
    out_specs = (tokens, tokens, P("dat", None), rows, rows, rows, rows, rows, P(None, ("dat", "seq")))
    return jax.shard_map(
        per_device, mesh=mesh, in_specs=in_specs, out_specs=out_specs, check_vma=False
    )
```
